256 devices in a mesh: prow: 16 (over z, x_hi), pcol: 16 (over x_lo, y, core).
Axes of the slice: x: 4 (x_hi: 2, x_lo: 2; x = x_hi * 2 + x_lo), y: 4, z: 8, core: 2. Of those that a mesh axis runs over, the one named last changes fastest.
Arguments:
- sigma_anc: float32 [6144, 6144], P('prow', 'pcol')
- panels: float32 [16384, 6144], P('pcol', 'prow'), may hold values from -0.8 to 0.8
- diag_blocks: float32 [32, 512, 512], P('pcol', 'prow'), may hold values from -6 to 6
- anc_blocks: int32 [32, 6], replicated, may hold values from 0 to 15, as said below
Outputs:
- cross_panel: float32 [16384, 6144], P('pcol', 'prow')
- diag_out: float32 [32, 512, 512], P('pcol', 'prow')
The draws below stay inside these ranges and needn't reach their ends.
Inputs may be any that keep to these rules, and one draw needn't show every extreme that they name: `anc_blocks`: each row holds 6 distinct block numbers.
All inputs are finite; a program needn't handle non-finite values.
Results may differ from the reference program's by a relative error of at most 0.000075.
Values sent between devices are 32-bit elements; how exact they have to be, the bound alone decides.
A program may use at most 128 MiB of HBM per device.

```python
import math
import jax
import jax.numpy as jnp
from jax import lax

W = 512
BLK = 384
NB = 16
K = 6
M = 6144
S = 32


def draw_sigma_anc(key, part):
    key = jax.random.fold_in(key, 7)
    key_one, key_two = jax.random.split(key, 2)
    noise = jax.random.normal(key_one, (M, M), jnp.float32)
    offdiag = (noise + noise.T) * (0.7071 / math.sqrt(K * BLK))
    diagonal = jax.random.uniform(key_two, (M,), jnp.float32, 0.5, 1.5)
    result = offdiag + jnp.eye(M, dtype=jnp.float32) * diagonal[None, :]
    return result


def draw_anc_blocks(key, part):
    key = jax.random.fold_in(key, 11)
    first = jnp.where(jnp.arange(S) % 2 == 0, NB - 1, 0).astype(jnp.int32)
    keys = jax.random.split(key, S)
    others = jax.vmap(lambda one_key: jax.random.permutation(one_key, NB - 1)[:K - 1])(keys).astype(jnp.int32)
    others = (first[:, None] + 1 + others) % NB
    return jnp.concatenate([first[:, None], others], axis=1).astype(jnp.int32)


def levels(own_key, extent, cuts, smallest, high):
    factor_of, own = 1.0, jax.random.fold_in(own_key, 6)
    for position, blocks in cuts:
        draws = jnp.exp(jax.random.uniform(jax.random.fold_in(own, position), (blocks,), jnp.float32, smallest / len(cuts), high / len(cuts)))
        factor_of = factor_of * jnp.repeat(draws, extent[position] // blocks).reshape([-1 if axis == position else 1 for axis in range(len(extent))])
    return factor_of


def scatter_about(key, extent, spread, reach, cuts=(), kind=jnp.bfloat16):
    entries = spread * jax.random.normal(key, extent, jnp.float32)
    if cuts:
        entries = entries * levels(key, extent, cuts, -0.22, 0.18)
    return jnp.clip(entries, -reach, reach).astype(kind)


def setup_inputs(seed: int = 0) -> dict:
    key_of = jax.random.split(jax.random.key(seed), 5)
    return {
        "sigma_anc": draw_sigma_anc(jax.random.fold_in(key_of[4], 71), 0),
        "panels": scatter_about(key_of[1], (S * W, M), 0.1, 0.8, ((0, 16), (1, 16)), jnp.float32),
        "diag_blocks": scatter_about(key_of[2], (S, W, W), 1.0, 6.0, ((0, 16), (1, 16)), jnp.float32),
        "anc_blocks": draw_anc_blocks(jax.random.fold_in(key_of[4], 71), 0),
    }


def reference(sigma_anc, panels, diag_blocks, anc_blocks):
    numbers = jnp.arange(NB, dtype=jnp.int32)
    member = jnp.any(anc_blocks[:, :, None] == numbers[None, None, :], axis=1).astype(jnp.float32)
    rowmask = jnp.repeat(jnp.repeat(member, W, axis=0), BLK, axis=1)
    masked = panels * rowmask
    image = jnp.dot(masked, sigma_anc, precision=lax.Precision.HIGHEST) * rowmask
    cross_panel = -image
    left_cube = masked.reshape(S, W, M)
    right_cube = image.reshape(S, W, M)
    diag_out = diag_blocks + jnp.einsum("swr,svr->swv", left_cube, right_cube, precision=lax.Precision.HIGHEST)
    return cross_panel, diag_out
```

```python
import functools

import jax
import jax.numpy as jnp
from jax import lax
from jax.experimental import pallas as pl
from jax.experimental.pallas import tpu as pltpu
from jax.sharding import PartitionSpec as P

W = 512
BLK = 384
NB = 16
K = 6
MESH = pl.DeviceIdType.MESH
F32 = jnp.float32
BF16 = jnp.bfloat16


def split(value):
    high = value.astype(BF16)
    return high, (value - high.astype(F32)).astype(BF16)


def kernel(
    anc, sig, pan, diag, cross, dout,
    abuf0, abuf1, pf0, pf1, sbuf, shi, slo, cacc, dbuf, drx, ebuf, drz,
    a_s, a_r, z_s, z_r, x_s, x_r, y_s, y_r, c_s, c_r, d_s, d_r, e_s, e_r,
):
    row, col = lax.axis_index("prow"), lax.axis_index("pcol")
    z, xh = row // 2, row % 2
    xl, y, core = col // 8, (col // 2) % 4, col % 2
    abuf, pf = (abuf0, abuf1), (pf0, pf1)

    def at_row(zz, xx):
        return (zz * 2 + xx, col)

    def at_col(ll, yy, cc):
        return (row, (ll * 4 + yy) * 2 + cc)

    def colnum(ll, yy, cc):
        return (ll * 4 + yy) * 2 + cc

    z_next = (at_row((z + 1) % 8, xh), at_row((z + 7) % 8, xh))
    x_pair = at_row(z, 1 - xh)
    l_pair = at_col(1 - xl, y, core)
    y_next = (at_col(xl, (y + 1) % 4, core), at_col(xl, (y + 3) % 4, core))
    c_pair = at_col(xl, y, 1 - core)
    row_peers = [((row + i) % 16, col) for i in range(1, 16)]

    barrier = pltpu.get_barrier_semaphore()
    peers = row_peers + [l_pair, *y_next, c_pair]
    for peer in peers:
        pl.semaphore_signal(barrier, inc=1, device_id=peer, device_id_type=MESH)
    pl.semaphore_wait(barrier, len(peers))

    sent = []

    def send(src, dst, ssem, rsem, peer):
        copy = pltpu.make_async_remote_copy(
            src_ref=src, dst_ref=dst, send_sem=ssem, recv_sem=rsem,
            device_id=peer, device_id_type=MESH,
        )
        copy.start()
        sent.append(copy)

    def arrived(dst, ssem, rsem, peer):
        pltpu.make_async_remote_copy(
            src_ref=dst, dst_ref=dst, send_sem=ssem, recv_sem=rsem,
            device_id=peer, device_id_type=MESH,
        ).wait_recv()

    for s in range(2):
        for i in range(1, 16):
            peer = (row + i) % 16
            send(pan.at[s, peer], abuf[s].at[row], a_s.at[s, i], a_r.at[s, i], (peer, col))
        abuf[s][pl.ds(row, 1)] = pan[s, pl.ds(row, 1)]

    sbuf[pl.ds(col, 1)] = sig[...].T[None]
    mine, pair = sbuf.at[col], sbuf.at[colnum(1 - xl, y, core)]
    send(mine, mine, y_s.at[6], y_r.at[6], l_pair)
    for d in range(2):
        send(mine, mine, y_s.at[d], y_r.at[d], y_next[d])
    send(mine, mine, c_s.at[0], c_r.at[0], c_pair)

    def sigma_pair():
        arrived(pair, y_s.at[6], y_r.at[6], l_pair)
        for d in range(2):
            send(pair, pair, y_s.at[2 + d], y_r.at[2 + d], y_next[d])
        send(pair, pair, c_s.at[1], c_r.at[1], c_pair)

    def sigma_near():
        for t in range(2):
            for d in range(2):
                block = sbuf.at[colnum(xl if t == 0 else 1 - xl, (y + (3 if d == 0 else 1)) % 4, core)]
                arrived(block, y_s.at[2 * t + d], y_r.at[2 * t + d], y_next[d])
                if t == d:
                    send(block, block, y_s.at[4 + t], y_r.at[4 + t], y_next[d])
                i = 2 + 2 * t + d
                send(block, block, c_s.at[i], c_r.at[i], c_pair)

    def sigma_far():
        for t in range(2):
            block = sbuf.at[colnum(xl if t == 0 else 1 - xl, (y + 2) % 4, core)]
            arrived(block, y_s.at[4 + t], y_r.at[4 + t], y_next[t])
            send(block, block, c_s.at[6 + t], c_r.at[6 + t], c_pair)

    def sigma_other_core():
        for i in range(8):
            t, yy = (
                (0, y), (1, y), (0, (y + 3) % 4), (0, (y + 1) % 4),
                (1, (y + 3) % 4), (1, (y + 1) % 4), (0, (y + 2) % 4), (1, (y + 2) % 4),
            )[i]
            block = sbuf.at[colnum(xl if t == 0 else 1 - xl, yy, 1 - core)]
            arrived(block, c_s.at[i], c_r.at[i], c_pair)

        def cut(i, carry):
            high, low = split(sbuf[i])
            shi[i] = high
            slo[i] = low
            return carry

        lax.fori_loop(0, NB, cut, 0)

    def compact(s):
        for i in range(1, 16):
            peer = (row + 16 - i) % 16
            arrived(abuf[s].at[peer], a_s.at[s, i], a_r.at[s, i], (peer, col))

        def take(k, carry):
            block = anc[2 * col + s, k]
            rows = abuf[s][block].reshape(2, 16, BLK)
            pf[s][0, pl.ds(row, 1), k] = rows[0][None]
            pf[s][1, pl.ds(row, 1), k] = rows[1][None]
            return carry

        lax.fori_loop(0, K, take, 0)

    def hops(s, kind, d):
        long = (s + (1 if kind == 2 else 0)) % 2
        return 4 if d == long else 3

    def piece(s, kind, zz):
        return pf[s].at[1 if kind == 1 else 0, zz * 2 + (1 - xh if kind == 2 else xh)]

    def z_send(s, kind, d, hop):
        block = piece(s, kind, (z + (8 - hop if d == 0 else hop)) % 8)
        send(block, block, z_s.at[s, kind, d, hop], z_r.at[s, kind, d, hop], z_next[d])

    def x_send(s, i, block):
        send(block, block, x_s.at[s, i], x_r.at[s, i], x_pair)

    def gather_start(s):
        x_send(s, 8, piece(s, 0, z))
        for kind in (0, 1):
            for d in range(2):
                z_send(s, kind, d, 0)
        x_send(s, 0, piece(s, 1, z))

    def gather_pair(s):
        arrived(piece(s, 2, z), x_s.at[s, 8], x_r.at[s, 8], x_pair)
        for d in range(2):
            z_send(s, 2, d, 0)

    def gather_hop(s, kind, hop):
        for d in range(2):
            if hop > hops(s, kind, d):
                continue
            block = piece(s, kind, (z + (8 - hop if d == 0 else hop)) % 8)
            arrived(block, z_s.at[s, kind, d, hop - 1], z_r.at[s, kind, d, hop - 1], z_next[d])
            if hop < hops(s, kind, d):
                z_send(s, kind, d, hop)
            if kind == 1:
                x_send(s, hop if d == 0 else 8 - hop, block)

    def gather_x(s):
        for i in range(8):
            block = pf[s].at[1, ((z + 8 - i) % 8) * 2 + 1 - xh]
            arrived(block, x_s.at[s, i], x_r.at[s, i], x_pair)

    def member(s):
        here = jnp.int32(0)
        for k in range(K):
            here = here + (anc[2 * col + s, k] == row).astype(jnp.int32)
        return here.astype(F32)

    def image(s, h):
        keep = member(s)
        cacc[...] = jnp.zeros_like(cacc)

        def term(k, carry):
            block = anc[2 * col + s, k]
            high, low = split(pf[s][h, :, k].reshape(256, BLK))
            s_high, s_low = shi[block], slo[block]
            cacc[...] += (
                jnp.dot(high, s_high, preferred_element_type=F32)
                + jnp.dot(low, s_high, preferred_element_type=F32)
                + jnp.dot(high, s_low, preferred_element_type=F32)
            )
            return carry

        lax.fori_loop(0, K, term, 0)
        rows = cacc[...] * keep
        cross[s, :, h] = -rows.reshape(16, 16, BLK)
        c_high, c_low = split(rows)
        p_high, p_low = split(pan[s].reshape(W, BLK) * keep)
        over = (((1,), (1,)), ((), ()))
        product = (
            lax.dot_general(c_high, p_high, over, preferred_element_type=F32)
            + lax.dot_general(c_low, p_high, over, preferred_element_type=F32)
            + lax.dot_general(c_high, p_low, over, preferred_element_type=F32)
        )
        dbuf[s, h] = product.reshape(8, 2, 16, W)
        send(dbuf.at[s, h, :, 1 - xh], drx.at[s, h], d_s.at[s, h], d_r.at[s, h], x_pair)

    def diag_z(s, h):
        arrived(drx.at[s, h], d_s.at[s, h], d_r.at[s, h], x_pair)
        ebuf[s, h] = dbuf[s, h, :, pl.ds(xh, 1)].reshape(8, 16, W) + drx[s, h]
        for i in range(1, 8):
            zz = (z + i) % 8
            send(ebuf.at[s, h, zz], drz.at[s, h, i], e_s.at[s, h, i], e_r.at[s, h, i], at_row(zz, xh))

    def diag_end(s, h):
        total = diag[s, h] + ebuf[s, h, pl.ds(z, 1)].reshape(16, W)
        for i in range(1, 8):
            arrived(drz.at[s, h, i], e_s.at[s, h, i], e_r.at[s, h, i], at_row((z + 8 - i) % 8, xh))
            total = total + drz[s, h, i]
        dout[s, h] = total

    sigma_pair()
    compact(0)
    gather_start(0)
    sigma_near()
    gather_pair(0)
    compact(1)
    for kind in (0, 1, 2):
        gather_hop(0, kind, 1)
    gather_start(1)
    sigma_far()
    for kind in (0, 1, 2):
        gather_hop(0, kind, 2)
    gather_pair(1)
    for hop in (3, 4):
        for kind in (0, 1, 2):
            gather_hop(0, kind, hop)
    sigma_other_core()
    for kind in (0, 1, 2):
        gather_hop(1, kind, 1)
    image(0, 0)
    for kind in (0, 1, 2):
        gather_hop(1, kind, 2)
    gather_x(0)
    image(0, 1)
    for kind in (0, 1, 2):
        gather_hop(1, kind, 3)
    diag_z(0, 0)
    diag_z(0, 1)
    for kind in (0, 1, 2):
        gather_hop(1, kind, 4)
    image(1, 0)
    gather_x(1)
    image(1, 1)
    diag_end(0, 0)
    diag_end(0, 1)
    diag_z(1, 0)
    diag_z(1, 1)
    diag_end(1, 0)
    diag_end(1, 1)
    for copy in sent:
        copy.wait_send()


def local(sigma_anc, panels, diag_blocks, anc_blocks):
    vmem = pl.BlockSpec(memory_space=pltpu.VMEM)
    dma = pltpu.SemaphoreType.DMA
    cross, dout = pl.pallas_call(
        kernel,
        out_shape=(
            jax.ShapeDtypeStruct((2, 16, 2, 16, BLK), F32),
            jax.ShapeDtypeStruct((2, 2, 16, W), F32),
        ),
        in_specs=[pl.BlockSpec(memory_space=pltpu.SMEM), vmem, vmem, vmem],
        out_specs=(vmem, vmem),
        scratch_shapes=[
            pltpu.VMEM((16, 32, BLK), F32),
            pltpu.VMEM((16, 32, BLK), F32),
            pltpu.VMEM((2, 16, K, 16, BLK), F32),
            pltpu.VMEM((2, 16, K, 16, BLK), F32),
            pltpu.VMEM((NB, BLK, BLK), F32),
            pltpu.VMEM((NB, BLK, BLK), BF16),
            pltpu.VMEM((NB, BLK, BLK), BF16),
            pltpu.VMEM((256, BLK), F32),
            pltpu.VMEM((2, 2, 8, 2, 16, W), F32),
            pltpu.VMEM((2, 2, 8, 16, W), F32),
            pltpu.VMEM((2, 2, 8, 16, W), F32),
            pltpu.VMEM((2, 2, 8, 16, W), F32),
            dma((2, 16)), dma((2, 16)),
            dma((2, 3, 2, 4)), dma((2, 3, 2, 4)),
            dma((2, 9)), dma((2, 9)),
            dma((7,)), dma((7,)),
            dma((8,)), dma((8,)),
            dma((2, 2)), dma((2, 2)),
            dma((2, 2, 8)), dma((2, 2, 8)),
        ],
        compiler_params=pltpu.CompilerParams(
            collective_id=0, has_side_effects=True, vmem_limit_bytes=56 << 20
        ),
    )(
        anc_blocks,
        sigma_anc,
        panels.reshape(2, 16, 32, BLK),
        diag_blocks.reshape(2, 2, 16, W),
    )
    return cross.reshape(2 * W, BLK), dout.reshape(2, 32, W)


def solution(mesh):
    placed = (P("prow", "pcol"), P("pcol", "prow"), P("pcol", "prow", None), P())
    return jax.shard_map(
        local,
        mesh=mesh,
        in_specs=placed,
        out_specs=(P("pcol", "prow"), P("pcol", "prow", None)),
        check_vma=False,
    )
```

```python
import jax
import jax.numpy as jnp
from jax import lax
from jax.experimental import pallas as pl
from jax.experimental.pallas import tpu as pltpu
from jax.sharding import PartitionSpec as P

W = 512
BLK = 384
NB = 16
K = 6
MESH = pl.DeviceIdType.MESH
F32 = jnp.float32
BF16 = jnp.bfloat16


def split(value):
    high = value.astype(BF16)
    return high, (value - high.astype(F32)).astype(BF16)


def kernel(
    anc, sig, pan, diag, cross, dout,
    abuf0, abuf1, pf0, pf1, sbuf, pbuf, cacc, cbuf, dbuf, drz,
    a_s, a_r, z_s, z_r, p_s, p_r, c_s, c_r, sx_s, sx_r, sy_s, sy_r, sc_s, sc_r, d_s, d_r,
):
    row, col = lax.axis_index("prow"), lax.axis_index("pcol")
    z, xh = row // 2, row % 2
    xl, y, core = col // 8, (col // 2) % 4, col % 2
    x = 2 * xh + xl
    abuf, pf = (abuf0, abuf1), (pf0, pf1)

    def at(xx, yy, zz, cc):
        return (zz * 2 + xx // 2, ((xx % 2) * 4 + yy) * 2 + cc)

    def sigma_block(xx, yy, cc):
        return sbuf.at[(xx // 2) * NB + ((xx % 2) * 4 + yy) * 2 + cc]

    x_next = (at((x + 1) % 4, y, z, core), at((x + 3) % 4, y, z, core))
    y_next = (at(x, (y + 1) % 4, z, core), at(x, (y + 3) % 4, z, core))
    z_next = (at(x, y, (z + 1) % 8, core), at(x, y, (z + 7) % 8, core))
    x_pair = at((x + 2) % 4, y, z, core)
    c_pair = at(x, y, z, 1 - core)

    sbuf[pl.ds(xh * NB + col, 1)] = sig[...].T[None]
    for s in range(2):
        abuf[s][pl.ds(row, 1)] = pan[s, pl.ds(row, 1)]

    barrier = pltpu.get_barrier_semaphore()
    peers = [((row + i) % 16, col) for i in range(1, 16)] + [*x_next, *y_next, c_pair]
    for peer in peers:
        pl.semaphore_signal(barrier, inc=1, device_id=peer, device_id_type=MESH)
    pl.semaphore_wait(barrier, len(peers))

    sent = []

    def send(src, dst, ssem, rsem, peer):
        copy = pltpu.make_async_remote_copy(
            src_ref=src, dst_ref=dst, send_sem=ssem, recv_sem=rsem,
            device_id=peer, device_id_type=MESH,
        )
        copy.start()
        sent.append(copy)

    def arrived(dst, ssem, rsem, peer):
        pltpu.make_async_remote_copy(
            src_ref=dst, dst_ref=dst, send_sem=ssem, recv_sem=rsem,
            device_id=peer, device_id_type=MESH,
        ).wait_recv()

    steps = (0, 3, 1, 2)

    def sigma_at(t, u, cc):
        return sigma_block((x + steps[t]) % 4, (y + steps[u]) % 4, cc)

    def sigma_core(t, u):
        block = sigma_at(t, u, core)
        send(block, block, sc_s.at[t, u], sc_r.at[t, u], c_pair)

    def sigma_y(t):
        block = sigma_at(t, 0, core)
        for d in range(2):
            send(block, block, sy_s.at[t, d], sy_r.at[t, d], y_next[d])

    def sigma_own():
        block = sigma_at(0, 0, core)
        for d in range(2):
            send(block, block, sx_s.at[d], sx_r.at[d], x_next[d])
        sigma_y(0)
        sigma_core(0, 0)

    def sigma_x_near():
        for d in range(2):
            block = sigma_at(1 + d, 0, core)
            arrived(block, sx_s.at[d], sx_r.at[d], x_next[d])

            @pl.when(core == d)
            def _():
                pltpu.make_async_remote_copy(
                    src_ref=block, dst_ref=block, send_sem=sx_s.at[2], recv_sem=sx_r.at[2],
                    device_id=x_next[d], device_id_type=MESH,
                ).start()

            sigma_y(1 + d)
            sigma_core(1 + d, 0)

    def sigma_x_far():
        block = sigma_at(3, 0, core)
        arrived(block, sx_s.at[2], sx_r.at[2], x_pair)
        sigma_y(3)
        sigma_core(3, 0)

    def sigma_y_near(t):
        for d in range(2):
            block = sigma_at(t, 1 + d, core)
            arrived(block, sy_s.at[t, d], sy_r.at[t, d], y_next[d])
            if d == t % 2:
                send(block, block, sy_s.at[t, 2], sy_r.at[t, 2], y_next[d])
            sigma_core(t, 1 + d)

    def sigma_y_far(t):
        block = sigma_at(t, 3, core)
        arrived(block, sy_s.at[t, 2], sy_r.at[t, 2], y_next[t % 2])
        sigma_core(t, 3)

    def sigma_other_core():
        for t in range(4):
            for u in range(4):
                arrived(sigma_at(t, u, 1 - core), sc_s.at[t, u], sc_r.at[t, u], c_pair)

    def rows_out(s):
        for i in range(1, 16):
            peer = (row + i) % 16
            send(pan.at[s, peer], abuf[s].at[row], a_s.at[s, i], a_r.at[s, i], (peer, col))

    def rows_in(s):
        for i in range(1, 16):
            peer = (row + 16 - i) % 16
            arrived(abuf[s].at[peer], a_s.at[s, i], a_r.at[s, i], (peer, col))

        def take(k, carry):
            block = anc[k, 2 * col + s]
            rows = abuf[s][block].reshape(2, 16, BLK)
            pf[s][0, pl.ds(z, 1), k] = rows[0][None]
            pf[s][1, pl.ds(z, 1), k] = rows[1][None]
            return carry

        lax.fori_loop(0, K, take, 0)
        for h in range(2):
            for d in range(2):
                z_send(s, h, d, 0)

    def hops(h, d):
        return 4 if d == h else 3

    def piece(s, h, d, hop):
        return pf[s].at[h, (z + (8 - hop if d == 0 else hop)) % 8]

    def z_send(s, h, d, hop):
        block = piece(s, h, d, hop)
        send(block, block, z_s.at[s, h, d, hop], z_r.at[s, h, d, hop], z_next[d])

    def ring(s, hop):
        for h in range(2):
            for d in range(2):
                if hop <= hops(h, d):
                    arrived(piece(s, h, d, hop), z_s.at[s, h, d, hop - 1], z_r.at[s, h, d, hop - 1], z_next[d])
                    if hop < hops(h, d):
                        z_send(s, h, d, hop)

    def pair_out(s):
        send(pan.at[s], pbuf.at[s], p_s.at[s], p_r.at[s], x_pair)

    def member(s, block):
        here = jnp.int32(0)
        for k in range(K):
            here = here + (anc[k, 2 * col + s] == block).astype(jnp.int32)
        return here.astype(F32)

    def image(s):
        cacc[...] = jnp.zeros_like(cacc)

        def term(k, carry):
            block = anc[k, 2 * col + s]
            high, low = split(pf[s][:, :, k].reshape(256, BLK))
            for n in range(2):
                s_high, s_low = split(sbuf[((xh + 1 + n) % 2) * NB + block])
                cacc[n] += (
                    jnp.dot(high, s_high, preferred_element_type=F32)
                    + jnp.dot(low, s_high, preferred_element_type=F32)
                    + jnp.dot(high, s_low, preferred_element_type=F32)
                )
            return carry

        lax.fori_loop(0, K, term, 0)
        other = cacc[0] * member(s, 2 * z + 1 - xh)
        cbuf[s] = -other.reshape(2, 8, 16, BLK)
        send(cbuf.at[s], cross.at[s, xh], c_s.at[s], c_r.at[s], x_pair)
        own = cacc[1] * member(s, row)
        cross[s, pl.ds(xh, 1)] = -own.reshape(1, 2, 8, 16, BLK)
        arrived(pbuf.at[s], p_s.at[s], p_r.at[s], x_pair)
        over = (((1,), (1,)), ((), ()))
        product = jnp.zeros((256, W), F32)
        for rows, panel in ((own, pan[s]), (other, pbuf[s])):
            high, low = split(rows)
            p_high, p_low = split(panel.reshape(W, BLK))
            product = product + (
                lax.dot_general(high, p_high, over, preferred_element_type=F32)
                + lax.dot_general(low, p_high, over, preferred_element_type=F32)
                + lax.dot_general(high, p_low, over, preferred_element_type=F32)
            )
        dbuf[s] = product.reshape(2, 8, 16, W)
        for i in (4, 3, 5, 2, 6, 1, 7):
            zz = (z + i) % 8
            send(dbuf.at[s, :, zz], drz.at[s, i], d_s.at[s, i], d_r.at[s, i], at(x, y, zz, core))

    def image_end(s):
        total = diag[s] + dbuf[s, :, pl.ds(z, 1)].reshape(2, 16, W)
        for i in range(1, 8):
            arrived(drz.at[s, i], d_s.at[s, i], d_r.at[s, i], at(x, y, (z + 8 - i) % 8, core))
            total = total + drz[s, i]
        dout[s] = total
        arrived(cross.at[s, 1 - xh], c_s.at[s], c_r.at[s], x_pair)

    sigma_own()
    rows_out(0)
    rows_out(1)
    sigma_x_near()
    rows_in(0)
    sigma_x_far()
    sigma_y_near(0)
    rows_in(1)
    pair_out(0)
    ring(0, 1)
    sigma_y_near(1)
    sigma_y_near(2)
    ring(0, 2)
    ring(1, 1)
    pair_out(1)
    sigma_y_near(3)
    ring(0, 3)
    ring(1, 2)
    sigma_y_far(0)
    sigma_y_far(1)
    ring(0, 4)
    ring(1, 3)
    sigma_y_far(2)
    sigma_y_far(3)
    sigma_other_core()
    image(0)
    ring(1, 4)
    image(1)
    image_end(0)
    image_end(1)
    for copy in sent:
        copy.wait_send()
    block = sigma_at(0, 0, core)
    pltpu.make_async_remote_copy(
        src_ref=block, dst_ref=block, send_sem=sx_s.at[2], recv_sem=sx_r.at[2],
        device_id=x_next[0], device_id_type=MESH,
    ).wait_send()


def local(sigma_anc, panels, diag_blocks, anc_blocks):
    vmem = pl.BlockSpec(memory_space=pltpu.VMEM)
    dma = pltpu.SemaphoreType.DMA
    cross, dout = pl.pallas_call(
        kernel,
        out_shape=(
            jax.ShapeDtypeStruct((2, 2, 2, 8, 16, BLK), F32),
            jax.ShapeDtypeStruct((2, 2, 16, W), F32),
        ),
        in_specs=[pl.BlockSpec(memory_space=pltpu.SMEM), vmem, vmem, vmem],
        out_specs=(vmem, vmem),
        scratch_shapes=[
            pltpu.VMEM((16, 32, BLK), F32),
            pltpu.VMEM((16, 32, BLK), F32),
            pltpu.VMEM((2, 8, K, 16, BLK), F32),
            pltpu.VMEM((2, 8, K, 16, BLK), F32),
            pltpu.VMEM((2 * NB, BLK, BLK), F32),
            pltpu.VMEM((2, 16, 32, BLK), F32),
            pltpu.VMEM((2, 256, BLK), F32),
            pltpu.VMEM((2, 2, 8, 16, BLK), F32),
            pltpu.VMEM((2, 2, 8, 16, W), F32),
            pltpu.VMEM((2, 8, 2, 16, W), F32),
            dma((2, 16)), dma((2, 16)),
            dma((2, 2, 2, 4)), dma((2, 2, 2, 4)),
            dma((2,)), dma((2,)),
            dma((2,)), dma((2,)),
            dma((3,)), dma((3,)),
            dma((4, 3)), dma((4, 3)),
            dma((4, 4)), dma((4, 4)),
            dma((2, 8)), dma((2, 8)),
        ],
        compiler_params=pltpu.CompilerParams(
            collective_id=0, has_side_effects=True, vmem_limit_bytes=56 << 20
        ),
    )(
        anc_blocks.T,
        sigma_anc,
        panels.reshape(2, 16, 32, BLK),
        diag_blocks.reshape(2, 2, 16, W),
    )
    cross = cross.transpose(0, 3, 1, 2, 4, 5)
    return cross.reshape(2 * W, BLK), dout.reshape(2, 32, W)


def solution(mesh):
    placed = (P("prow", "pcol"), P("pcol", "prow"), P("pcol", "prow", None), P())
    return jax.shard_map(
        local,
        mesh=mesh,
        in_specs=placed,
        out_specs=(P("pcol", "prow"), P("pcol", "prow", None)),
        check_vma=False,
    )
```

```python
import jax
import jax.numpy as jnp
from jax import lax
from jax.experimental import pallas as pl
from jax.experimental.pallas import tpu as pltpu
from jax.sharding import PartitionSpec as P

W = 512
BLK = 384
NB = 16
K = 6
MESH = pl.DeviceIdType.MESH
F32 = jnp.float32
BF16 = jnp.bfloat16


def split(value):
    high = value.astype(BF16)
    return high, (value - high.astype(F32)).astype(BF16)


def kernel(
    anc, sig, pan, diag, cross, dout,
    abuf0, abuf1, pf0, pf1, sbuf, pbuf, cacc, cbuf, dbuf, drz,
    a_s, a_r, z_s, z_r, p_s, p_r, c_s, c_r, sx_s, sx_r, sy_s, sy_r, sc_s, sc_r, d_s, d_r,
):
    row, col = lax.axis_index("prow"), lax.axis_index("pcol")
    z, xh = row // 2, row % 2
    xl, y, core = col // 8, (col // 2) % 4, col % 2
    x = 2 * xh + xl
    abuf, pf = (abuf0, abuf1), (pf0, pf1)

    def at(xx, yy, zz, cc):
        return (zz * 2 + xx // 2, ((xx % 2) * 4 + yy) * 2 + cc)

    def sigma_block(xx, yy, cc):
        return sbuf.at[(xx // 2) * NB + ((xx % 2) * 4 + yy) * 2 + cc]

    x_next = (at((x + 1) % 4, y, z, core), at((x + 3) % 4, y, z, core))
    y_next = (at(x, (y + 1) % 4, z, core), at(x, (y + 3) % 4, z, core))
    z_next = (at(x, y, (z + 1) % 8, core), at(x, y, (z + 7) % 8, core))
    x_pair = at((x + 2) % 4, y, z, core)
    c_pair = at(x, y, z, 1 - core)

    sbuf[pl.ds(xh * NB + col, 1)] = sig[...].T[None]
    for s in range(2):
        abuf[s][pl.ds(row, 1)] = pan[s, pl.ds(z, 1), pl.ds(xh, 1)].reshape(1, 32, BLK)

    barrier = pltpu.get_barrier_semaphore()
    peers = [((row + i) % 16, col) for i in range(1, 16)] + [*x_next, *y_next, c_pair]
    for peer in peers:
        pl.semaphore_signal(barrier, inc=1, device_id=peer, device_id_type=MESH)
    pl.semaphore_wait(barrier, len(peers))

    sent = []

    def send(src, dst, ssem, rsem, peer):
        copy = pltpu.make_async_remote_copy(
            src_ref=src, dst_ref=dst, send_sem=ssem, recv_sem=rsem,
            device_id=peer, device_id_type=MESH,
        )
        copy.start()
        sent.append(copy)

    def arrived(dst, ssem, rsem, peer):
        pltpu.make_async_remote_copy(
            src_ref=dst, dst_ref=dst, send_sem=ssem, recv_sem=rsem,
            device_id=peer, device_id_type=MESH,
        ).wait_recv()

    steps = (0, 3, 1, 2)

    def sigma_at(t, u, cc):
        return sigma_block((x + steps[t]) % 4, (y + steps[u]) % 4, cc)

    def sigma_core(t, u):
        block = sigma_at(t, u, core)
        send(block, block, sc_s.at[t, u], sc_r.at[t, u], c_pair)

    def sigma_y(t):
        block = sigma_at(t, 0, core)
        for d in range(2):
            send(block, block, sy_s.at[t, d], sy_r.at[t, d], y_next[d])

    def sigma_x(u):
        block = sigma_at(0, u, core)
        for d in range(2):
            send(block, block, sx_s.at[u // 3, d], sx_r.at[u // 3, d], x_next[d])

    def far(block, ssem, rsem, peers, d):
        @pl.when(core == d)
        def _():
            pltpu.make_async_remote_copy(
                src_ref=block, dst_ref=block, send_sem=ssem, recv_sem=rsem,
                device_id=peers[d], device_id_type=MESH,
            ).start()

    def sigma_own():
        sigma_x(0)
        sigma_y(0)
        sigma_core(0, 0)

    def sigma_x_near(u):
        for d in range(2):
            block = sigma_at(1 + d, u, core)
            arrived(block, sx_s.at[u // 3, d], sx_r.at[u // 3, d], x_next[d])
            far(block, sx_s.at[u // 3, 2], sx_r.at[u // 3, 2], x_next, d)
            if u == 0:
                sigma_y(1 + d)
            sigma_core(1 + d, u)

    def sigma_x_far(u):
        block = sigma_at(3, u, core)
        arrived(block, sx_s.at[u // 3, 2], sx_r.at[u // 3, 2], x_pair)
        if u == 0:
            sigma_y(3)
        sigma_core(3, u)

    def sigma_y_near(t):
        for d in range(2):
            block = sigma_at(t, 1 + d, core)
            arrived(block, sy_s.at[t, d], sy_r.at[t, d], y_next[d])
            if t == 0:
                far(block, sy_s.at[0, 2], sy_r.at[0, 2], y_next, d)
            sigma_core(t, 1 + d)

    def sigma_y_far():
        block = sigma_at(0, 3, core)
        arrived(block, sy_s.at[0, 2], sy_r.at[0, 2], y_next[0])
        sigma_x(3)
        sigma_core(0, 3)

    def sigma_other_core():
        for t in range(4):
            for u in range(4):
                arrived(sigma_at(t, u, 1 - core), sc_s.at[t, u], sc_r.at[t, u], c_pair)

    def sigma_end():
        block = sigma_at(0, 0, core)
        for ssem, rsem in ((sx_s.at[0, 2], sx_r.at[0, 2]), (sx_s.at[1, 2], sx_r.at[1, 2]), (sy_s.at[0, 2], sy_r.at[0, 2])):
            pltpu.make_async_remote_copy(
                src_ref=block, dst_ref=block, send_sem=ssem, recv_sem=rsem,
                device_id=c_pair, device_id_type=MESH,
            ).wait_send()

    def rows_out(s):
        for i in range(1, 16):
            peer = (row + i) % 16
            send(pan.at[s, peer // 2, peer % 2], abuf[s].at[row], a_s.at[s, i], a_r.at[s, i], (peer, col))

    def rows_in(s):
        for i in range(1, 16):
            peer = (row + 16 - i) % 16
            arrived(abuf[s].at[peer], a_s.at[s, i], a_r.at[s, i], (peer, col))

        def take(k, carry):
            block = anc[k, 2 * col + s]
            rows = abuf[s][block].reshape(2, 16, BLK)
            pf[s][0, pl.ds(z, 1), k] = rows[0][None]
            pf[s][1, pl.ds(z, 1), k] = rows[1][None]
            return carry

        lax.fori_loop(0, K, take, 0)

    def ring_start(s):
        for h in range(2):
            for d in range(2):
                z_send(s, h, d, 0)

    def hops(h, d):
        return 4 if d == h else 3

    def piece(s, h, d, hop):
        return pf[s].at[h, (z + (8 - hop if d == 0 else hop)) % 8]

    def z_send(s, h, d, hop):
        block = piece(s, h, d, hop)
        send(block, block, z_s.at[s, h, d, hop], z_r.at[s, h, d, hop], z_next[d])

    def ring(s, hop):
        for h in range(2):
            for d in range(2):
                if hop <= hops(h, d):
                    arrived(piece(s, h, d, hop), z_s.at[s, h, d, hop - 1], z_r.at[s, h, d, hop - 1], z_next[d])
                    if hop < hops(h, d):
                        z_send(s, h, d, hop)

    def pair_out(s):
        send(pan.at[s, :, xh], pbuf.at[s, :, xh], p_s.at[s], p_r.at[s], x_pair)

    def member(s, block):
        here = jnp.int32(0)
        for k in range(K):
            here = here + (anc[k, 2 * col + s] == block).astype(jnp.int32)
        return here.astype(F32)

    def image(s):
        cacc[...] = jnp.zeros_like(cacc)

        def term(k, carry):
            block = anc[k, 2 * col + s]
            high, low = split(pf[s][:, :, k].reshape(256, BLK))
            for n in range(2):
                s_high, s_low = split(sbuf[((xh + 1 + n) % 2) * NB + block])
                cacc[n] += (
                    jnp.dot(high, s_high, preferred_element_type=F32)
                    + jnp.dot(low, s_high, preferred_element_type=F32)
                    + jnp.dot(high, s_low, preferred_element_type=F32)
                )
            return carry

        lax.fori_loop(0, K, term, 0)
        other = cacc[0] * member(s, 2 * z + 1 - xh)
        cbuf[s] = -other.reshape(2, 8, 16, BLK)
        send(cbuf.at[s], cross.at[s, xh], c_s.at[s], c_r.at[s], x_pair)
        own = cacc[1] * member(s, row)
        cross[s, pl.ds(xh, 1)] = -own.reshape(1, 2, 8, 16, BLK)
        mine = jnp.zeros((2, 8, 16, BLK), F32)
        for k in range(K):
            mine = mine + pf[s][:, :, k] * (anc[k, 2 * col + s] == 2 * z + 1 - xh).astype(F32)
        for h in range(2):
            pbuf[s, :, pl.ds(xh, 1), 16 * h : 16 * h + 16] = mine[h].reshape(8, 1, 16, BLK)
        arrived(pbuf.at[s, :, 1 - xh], p_s.at[s], p_r.at[s], x_pair)
        over = (((1,), (1,)), ((), ()))
        product = jnp.zeros((256, W), F32)
        for rows, panel in ((own, pan[s]), (other, pbuf[s])):
            high, low = split(rows)
            p_high, p_low = split(panel.reshape(W, BLK))
            product = product + (
                lax.dot_general(high, p_high, over, preferred_element_type=F32)
                + lax.dot_general(low, p_high, over, preferred_element_type=F32)
                + lax.dot_general(high, p_low, over, preferred_element_type=F32)
            )
        dbuf[s] = product.reshape(2, 8, 16, W)
        for i in (4, 3, 5, 2, 6, 1, 7):
            zz = (z + i) % 8
            send(dbuf.at[s, :, zz], drz.at[s, i], d_s.at[s, i], d_r.at[s, i], at(x, y, zz, core))

    def image_end(s):
        total = diag[s] + dbuf[s, :, pl.ds(z, 1)].reshape(2, 16, W)
        for i in range(1, 8):
            arrived(drz.at[s, i], d_s.at[s, i], d_r.at[s, i], at(x, y, (z + 8 - i) % 8, core))
            total = total + drz[s, i]
        dout[s] = total
        arrived(cross.at[s, 1 - xh], c_s.at[s], c_r.at[s], x_pair)

    sigma_own()
    rows_out(0)
    rows_out(1)
    sigma_y_near(0)
    sigma_x_near(0)
    rows_in(0)
    ring_start(0)
    sigma_x_far(0)
    sigma_y_far()
    sigma_y_near(1)
    rows_in(1)
    ring(0, 1)
    ring_start(1)
    sigma_x_near(3)
    sigma_y_near(2)
    ring(0, 2)
    sigma_x_far(3)
    pair_out(0)
    ring(0, 3)
    ring(1, 1)
    sigma_y_near(3)
    ring(0, 4)
    ring(1, 2)
    sigma_other_core()
    pair_out(1)
    image(0)
    ring(1, 3)
    ring(1, 4)
    image(1)
    image_end(0)
    image_end(1)
    for copy in sent:
        copy.wait_send()
    sigma_end()


def local(sigma_anc, panels, diag_blocks, anc_blocks):
    vmem = pl.BlockSpec(memory_space=pltpu.VMEM)
    dma = pltpu.SemaphoreType.DMA
    cross, dout = pl.pallas_call(
        kernel,
        out_shape=(
            jax.ShapeDtypeStruct((2, 2, 2, 8, 16, BLK), F32),
            jax.ShapeDtypeStruct((2, 2, 16, W), F32),
        ),
        in_specs=[pl.BlockSpec(memory_space=pltpu.SMEM), vmem, vmem, vmem],
        out_specs=(vmem, vmem),
        scratch_shapes=[
            pltpu.VMEM((16, 32, BLK), F32),
            pltpu.VMEM((16, 32, BLK), F32),
            pltpu.VMEM((2, 8, K, 16, BLK), F32),
            pltpu.VMEM((2, 8, K, 16, BLK), F32),
            pltpu.VMEM((2 * NB, BLK, BLK), F32),
            pltpu.VMEM((2, 8, 2, 32, BLK), F32),
            pltpu.VMEM((2, 256, BLK), F32),
            pltpu.VMEM((2, 2, 8, 16, BLK), F32),
            pltpu.VMEM((2, 2, 8, 16, W), F32),
            pltpu.VMEM((2, 8, 2, 16, W), F32),
            dma((2, 16)), dma((2, 16)),
            dma((2, 2, 2, 4)), dma((2, 2, 2, 4)),
            dma((2,)), dma((2,)),
            dma((2,)), dma((2,)),
            dma((2, 3)), dma((2, 3)),
            dma((4, 3)), dma((4, 3)),
            dma((4, 4)), dma((4, 4)),
            dma((2, 8)), dma((2, 8)),
        ],
        compiler_params=pltpu.CompilerParams(
            collective_id=0, has_side_effects=True, vmem_limit_bytes=56 << 20
        ),
    )(
        anc_blocks.T,
        sigma_anc,
        panels.reshape(2, 8, 2, 32, BLK),
        diag_blocks.reshape(2, 2, 16, W),
    )
    cross = cross.transpose(0, 3, 1, 2, 4, 5)
    return cross.reshape(2 * W, BLK), dout.reshape(2, 32, W)


def solution(mesh):
    placed = (P("prow", "pcol"), P("pcol", "prow"), P("pcol", "prow", None), P())
    return jax.shard_map(
        local,
        mesh=mesh,
        in_specs=placed,
        out_specs=(P("pcol", "prow"), P("pcol", "prow", None)),
        check_vma=False,
    )
```

```python
import jax
import jax.numpy as jnp
from jax import lax
from jax.experimental import pallas as pl
from jax.experimental.pallas import tpu as pltpu
from jax.sharding import PartitionSpec as P

W = 512
BLK = 384
NB = 16
K = 6
MESH = pl.DeviceIdType.MESH
F32 = jnp.float32
BF16 = jnp.bfloat16


def split(value):
    high = value.astype(BF16)
    return high, (value - high.astype(F32)).astype(BF16)


def kernel(
    anc, sig, pan, diag, cross, dout,
    abuf0, abuf1, pf0, pf1, s_own, s_oth, pbuf, cacc, cbuf, dbuf, drz,
    a_s, a_r, z_s, z_r, p_s, p_r, c_s, c_r, sx_s, sx_r, sy_s, sy_r, sc_s, sc_r, d_s, d_r,
):
    row, col = lax.axis_index("prow"), lax.axis_index("pcol")
    z, xh = row // 2, row % 2
    xl, y, core = col // 8, (col // 2) % 4, col % 2
    x = 2 * xh + xl
    abuf, pf = (abuf0, abuf1), (pf0, pf1)

    def at(xx, yy, zz, cc):
        return (zz * 2 + xx // 2, ((xx % 2) * 4 + yy) * 2 + cc)

    x_same, x_cross = (x + 1 + 2 * xl) % 4, (x + 3 + 2 * xl) % 4
    x_next = (at(x_same, y, z, core), at(x_cross, y, z, core))
    y_next = (at(x, (y + 1) % 4, z, core), at(x, (y + 3) % 4, z, core))
    z_next = (at(x, y, (z + 1) % 8, core), at(x, y, (z + 7) % 8, core))
    x_pair = at((x + 2) % 4, y, z, core)
    c_pair = at(x, y, z, 1 - core)

    s_own[pl.ds(col, 1)] = sig[...].T[None]
    for s in range(2):
        abuf[s][pl.ds(row, 1)] = pan[s, pl.ds(z, 1), pl.ds(xh, 1)].reshape(1, 32, BLK)

    barrier = pltpu.get_barrier_semaphore()
    peers = [((row + i) % 16, col) for i in range(1, 16)] + [*x_next, *y_next, c_pair]
    for peer in peers:
        pl.semaphore_signal(barrier, inc=1, device_id=peer, device_id_type=MESH)
    pl.semaphore_wait(barrier, len(peers))

    sent = []

    def send(src, dst, ssem, rsem, peer):
        copy = pltpu.make_async_remote_copy(
            src_ref=src, dst_ref=dst, send_sem=ssem, recv_sem=rsem,
            device_id=peer, device_id_type=MESH,
        )
        copy.start()
        sent.append(copy)

    def arrived(dst, ssem, rsem, peer):
        pltpu.make_async_remote_copy(
            src_ref=dst, dst_ref=dst, send_sem=ssem, recv_sem=rsem,
            device_id=peer, device_id_type=MESH,
        ).wait_recv()

    def sigma_at(t, u, cc, owner=None):
        xx = (x, x_same, x_cross, (x + 2) % 4)[t]
        yy = (y + (0, 3, 1, 2)[u]) % 4
        owner = t < 2 if owner is None else owner
        return (s_own if owner else s_oth).at[((xx % 2) * 4 + yy) * 2 + cc]

    def sigma_core(t, u):
        block = sigma_at(t, u, core)
        send(block, block, sc_s.at[t, u], sc_r.at[t, u], c_pair)

    def sigma_y(t):
        block = sigma_at(t, 0, core)
        for d in range(2):
            send(block, block, sy_s.at[t, d], sy_r.at[t, d], y_next[d])

    def sigma_x(u):
        for d in range(2):
            send(sigma_at(0, u, core), sigma_at(0, u, core, d == 0), sx_s.at[u // 3, d], sx_r.at[u // 3, d], x_next[d])

    def far(src, dst, ssem, rsem, peer, d):
        @pl.when(core == d)
        def _():
            pltpu.make_async_remote_copy(
                src_ref=src, dst_ref=dst, send_sem=ssem, recv_sem=rsem,
                device_id=peer, device_id_type=MESH,
            ).start()

    def sigma_first():
        sigma_x(0)
        sigma_y(0)
        sigma_core(0, 0)

    def sigma_x_near(u):
        for d in range(2):
            block = sigma_at(1 + d, u, core)
            arrived(block, sx_s.at[u // 3, d], sx_r.at[u // 3, d], x_next[d])
            far(block, sigma_at(1 + d, u, core, False), sx_s.at[u // 3, 2], sx_r.at[u // 3, 2], x_next[1 - d], d)
            if u == 0:
                sigma_y(1 + d)
            sigma_core(1 + d, u)

    def sigma_x_far(u):
        block = sigma_at(3, u, core)
        arrived(block, sx_s.at[u // 3, 2], sx_r.at[u // 3, 2], x_pair)
        if u == 0:
            sigma_y(3)
        sigma_core(3, u)

    def sigma_y_near(t):
        for d in range(2):
            block = sigma_at(t, 1 + d, core)
            arrived(block, sy_s.at[t, d], sy_r.at[t, d], y_next[d])
            if t == 0:
                far(block, block, sy_s.at[0, 2], sy_r.at[0, 2], y_next[d], d)
            sigma_core(t, 1 + d)

    def sigma_y_far():
        block = sigma_at(0, 3, core)
        arrived(block, sy_s.at[0, 2], sy_r.at[0, 2], y_next[0])
        sigma_x(3)
        sigma_core(0, 3)

    def sigma_ready(n):
        for t in ((2, 3), (0, 1))[n]:
            for u in range(4):
                arrived(sigma_at(t, u, 1 - core), sc_s.at[t, u], sc_r.at[t, u], c_pair)

    def sigma_end():
        block = sigma_at(0, 0, core)
        for ssem, rsem in ((sx_s.at[0, 2], sx_r.at[0, 2]), (sx_s.at[1, 2], sx_r.at[1, 2]), (sy_s.at[0, 2], sy_r.at[0, 2])):
            pltpu.make_async_remote_copy(
                src_ref=block, dst_ref=block, send_sem=ssem, recv_sem=rsem,
                device_id=c_pair, device_id_type=MESH,
            ).wait_send()

    def rows_out(s):
        for i in (8, 6, 10, 4, 12, 2, 14, 7, 9, 5, 11, 3, 13, 1, 15):
            peer = (row + i) % 16
            send(pan.at[s, peer // 2, peer % 2], abuf[s].at[row], a_s.at[s, i], a_r.at[s, i], (peer, col))

    def rows_in(s):
        for i in range(1, 16):
            peer = (row + 16 - i) % 16
            arrived(abuf[s].at[peer], a_s.at[s, i], a_r.at[s, i], (peer, col))

        def take(k, carry):
            block = anc[k, 2 * col + s]
            rows = abuf[s][block].reshape(2, 16, BLK)
            pf[s][0, pl.ds(z, 1), k] = rows[0][None]
            pf[s][1, pl.ds(z, 1), k] = rows[1][None]
            return carry

        lax.fori_loop(0, K, take, 0)

    def ring_start(s):
        for h in range(2):
            for d in range(2):
                z_send(s, h, d, 0)

    def hops(h, d):
        return 4 if d == h else 3

    def piece(s, h, d, hop):
        return pf[s].at[h, (z + (8 - hop if d == 0 else hop)) % 8]

    def z_send(s, h, d, hop):
        block = piece(s, h, d, hop)
        send(block, block, z_s.at[s, h, d, hop], z_r.at[s, h, d, hop], z_next[d])

    def ring(s, hop):
        for h in range(2):
            for d in range(2):
                if hop <= hops(h, d):
                    arrived(piece(s, h, d, hop), z_s.at[s, h, d, hop - 1], z_r.at[s, h, d, hop - 1], z_next[d])
                    if hop < hops(h, d):
                        z_send(s, h, d, hop)

    def pair_out(s):
        send(pan.at[s, :, xh], pbuf.at[s, :, xh], p_s.at[s], p_r.at[s], x_pair)

    def member(s, block):
        here = jnp.int32(0)
        for k in range(K):
            here = here + (anc[k, 2 * col + s] == block).astype(jnp.int32)
        return here.astype(F32)

    def image(s):
        def term(k, carry):
            high, low, s_high, s_low = [], [], [], []
            for i in range(2):
                block = anc[2 * k + i, 2 * col + s]
                p_high, p_low = split(pf[s][:, :, 2 * k + i].reshape(256, BLK))
                high.append(p_high)
                low.append(p_low)
                for rows in (s_oth, s_own):
                    r_high, r_low = split(rows[block])
                    s_high.append(r_high)
                    s_low.append(r_low)
            left = jnp.concatenate(high + low + high, axis=1)
            right = jnp.concatenate(
                [jnp.concatenate(s_high[n::2] + s_high[n::2] + s_low[n::2], axis=0) for n in range(2)], axis=1
            )
            part = jnp.dot(left, right, preferred_element_type=F32)
            for n in range(2):
                cacc[n] = jnp.where(k == 0, 0.0, cacc[n]) + part[:, n * BLK : (n + 1) * BLK]
            return carry

        lax.fori_loop(0, K // 2, term, 0)
        other = cacc[0] * member(s, 2 * z + 1 - xh)
        cacc[0] = other
        cbuf[s] = -other.reshape(2, 8, 16, BLK)
        send(cbuf.at[s], cross.at[s, xh], c_s.at[s], c_r.at[s], x_pair)
        own = cacc[1] * member(s, row)
        cacc[1] = own
        cross[s, pl.ds(xh, 1)] = -own.reshape(1, 2, 8, 16, BLK)

    def image_out(s):
        mine = jnp.zeros((2, 8, 16, BLK), F32)
        for k in range(K):
            mine = mine + pf[s][:, :, k] * (anc[k, 2 * col + s] == 2 * z + 1 - xh).astype(F32)
        for h in range(2):
            pbuf[s, :, pl.ds(xh, 1), 16 * h : 16 * h + 16] = mine[h].reshape(8, 1, 16, BLK)
        arrived(pbuf.at[s, :, 1 - xh], p_s.at[s], p_r.at[s], x_pair)
        over = (((1,), (1,)), ((), ()))
        left, right = [], []
        for rows, panel in ((cacc[1], pan[s]), (cacc[0], pbuf[s])):
            high, low = split(rows)
            p_high, p_low = split(panel.reshape(W, BLK))
            left += [high, low, high]
            right += [p_high, p_high, p_low]
        product = lax.dot_general(
            jnp.concatenate(left, axis=1), jnp.concatenate(right, axis=1),
            (((1,), (1,)), ((), ())), preferred_element_type=F32,
        )
        dbuf[s] = product.reshape(2, 8, 16, W)
        sums(s, 0)

    def sums(s, hop):
        for h in range(2):
            for d in range(2):
                if hop >= hops(h, d):
                    continue
                away = hops(h, d) - hop
                own = dbuf.at[s, h, (z + (away if d == 0 else 8 - away)) % 8]
                if hop > 0:
                    slot = drz.at[s, h, d, hop - 1]
                    arrived(slot, d_s.at[s, h, d, hop - 1], d_r.at[s, h, d, hop - 1], z_next[d])
                    slot[...] += own[...]
                    own = slot
                send(own, drz.at[s, h, d, hop], d_s.at[s, h, d, hop], d_r.at[s, h, d, hop], z_next[d])

    def sums_end(s):
        for h in range(2):
            total = diag[s, h] + dbuf[s, h, pl.ds(z, 1)].reshape(16, W)
            for d in range(2):
                hop = hops(h, d) - 1
                arrived(drz.at[s, h, d, hop], d_s.at[s, h, d, hop], d_r.at[s, h, d, hop], z_next[d])
                total = total + drz[s, h, d, hop]
            dout[s, h] = total
        arrived(cross.at[s, 1 - xh], c_s.at[s], c_r.at[s], x_pair)

    sigma_first()
    rows_out(0)
    rows_out(1)
    sigma_y_near(0)
    sigma_x_near(0)
    rows_in(0)
    ring_start(0)
    sigma_x_far(0)
    sigma_y_far()
    rows_in(1)
    ring_start(1)
    ring(0,1)
    sigma_y_near(1)
    ring(1,1)
    sigma_x_near(3)
    ring(0,2)
    sigma_y_near(2)
    ring(1,2)
    sigma_x_far(3)
    pair_out(0)
    ring(0,3)
    sigma_y_near(3)
    ring(1,3)
    pair_out(1)
    ring(0,4)
    sigma_ready(1)
    sigma_ready(0)
    image(0)
    image_out(0)
    ring(1,4)
    image(1)
    sums(0,1)
    image_out(1)
    sums(0,2)
    sums(1,1)
    sums(0,3)
    sums(1,2)
    sums(1,3)
    sums_end(0)
    sums_end(1)
    for copy in sent:
        copy.wait_send()
    sigma_end()


def local(sigma_anc, panels, diag_blocks, anc_blocks):
    vmem = pl.BlockSpec(memory_space=pltpu.VMEM)
    dma = pltpu.SemaphoreType.DMA
    cross, dout = pl.pallas_call(
        kernel,
        out_shape=(
            jax.ShapeDtypeStruct((2, 2, 2, 8, 16, BLK), F32),
            jax.ShapeDtypeStruct((2, 2, 16, W), F32),
        ),
        in_specs=[pl.BlockSpec(memory_space=pltpu.SMEM), vmem, vmem, vmem],
        out_specs=(vmem, vmem),
        scratch_shapes=[
            pltpu.VMEM((16, 32, BLK), F32),
            pltpu.VMEM((16, 32, BLK), F32),
            pltpu.VMEM((2, 8, K, 16, BLK), F32),
            pltpu.VMEM((2, 8, K, 16, BLK), F32),
            pltpu.VMEM((NB, BLK, BLK), F32),
            pltpu.VMEM((NB, BLK, BLK), F32),
            pltpu.VMEM((2, 8, 2, 32, BLK), F32),
            pltpu.VMEM((2, 256, BLK), F32),
            pltpu.VMEM((2, 2, 8, 16, BLK), F32),
            pltpu.VMEM((2, 2, 8, 16, W), F32),
            pltpu.VMEM((2, 2, 2, 4, 16, W), F32),
            dma((2, 16)), dma((2, 16)),
            dma((2, 2, 2, 4)), dma((2, 2, 2, 4)),
            dma((2,)), dma((2,)),
            dma((2,)), dma((2,)),
            dma((2, 3)), dma((2, 3)),
            dma((4, 3)), dma((4, 3)),
            dma((4, 4)), dma((4, 4)),
            dma((2, 2, 2, 4)), dma((2, 2, 2, 4)),
        ],
        compiler_params=pltpu.CompilerParams(
            collective_id=0, has_side_effects=True, vmem_limit_bytes=56 << 20
        ),
    )(
        anc_blocks.T,
        sigma_anc,
        panels.reshape(2, 8, 2, 32, BLK),
        diag_blocks.reshape(2, 2, 16, W),
    )
    cross = cross.transpose(0, 3, 1, 2, 4, 5)
    return cross.reshape(2 * W, BLK), dout.reshape(2, 32, W)


def solution(mesh):
    placed = (P("prow", "pcol"), P("pcol", "prow"), P("pcol", "prow", None), P())
    return jax.shard_map(
        local,
        mesh=mesh,
        in_specs=placed,
        out_specs=(P("pcol", "prow"), P("pcol", "prow", None)),
        check_vma=False,
    )
```

```python
import jax
import jax.numpy as jnp
from jax import lax
from jax.experimental import pallas as pl
from jax.experimental.pallas import tpu as pltpu
from jax.sharding import PartitionSpec as P

W = 512
BLK = 384
NB = 16
K = 6
MESH = pl.DeviceIdType.MESH
F32 = jnp.float32
BF16 = jnp.bfloat16


def split(value):
    high = value.astype(BF16)
    return high, (value - high.astype(F32)).astype(BF16)


def kernel(
    anc, sig, pan, diag, cross, dout,
    abuf0, abuf1, pf0, pf1, s_own, s_oth, pbuf, cacc, cbuf, dbuf, drz, p_hi, p_lo,
    a_s, a_r, z_s, z_r, p_s, p_r, c_s, c_r, sx_s, sx_r, sy_s, sy_r, sc_s, sc_r, d_s, d_r,
):
    row, col = lax.axis_index("prow"), lax.axis_index("pcol")
    z, xh = row // 2, row % 2
    xl, y, core = col // 8, (col // 2) % 4, col % 2
    x = 2 * xh + xl
    abuf, pf = (abuf0, abuf1), (pf0, pf1)

    def at(xx, yy, zz, cc):
        return (zz * 2 + xx // 2, ((xx % 2) * 4 + yy) * 2 + cc)

    x_same, x_cross = (x + 1 + 2 * xl) % 4, (x + 3 + 2 * xl) % 4
    x_next = (at(x_same, y, z, core), at(x_cross, y, z, core))
    y_next = (at(x, (y + 1) % 4, z, core), at(x, (y + 3) % 4, z, core))
    z_next = (at(x, y, (z + 1) % 8, core), at(x, y, (z + 7) % 8, core))
    x_pair = at((x + 2) % 4, y, z, core)
    c_pair = at(x, y, z, 1 - core)

    s_own[pl.ds(col, 1)] = sig[...].T[None]
    for s in range(2):
        abuf[s][pl.ds(row, 1)] = pan[s, pl.ds(z, 1), pl.ds(xh, 1)].reshape(1, 32, BLK)

    for s in range(2):
        p_hi[s], p_lo[s] = split(pan[s].reshape(W, BLK))

    barrier = pltpu.get_barrier_semaphore()
    peers = [((row + i) % 16, col) for i in range(1, 16)] + [*x_next, *y_next, c_pair]
    for peer in peers:
        pl.semaphore_signal(barrier, inc=1, device_id=peer, device_id_type=MESH)
    pl.semaphore_wait(barrier, len(peers))

    sent = []

    def send(src, dst, ssem, rsem, peer):
        copy = pltpu.make_async_remote_copy(
            src_ref=src, dst_ref=dst, send_sem=ssem, recv_sem=rsem,
            device_id=peer, device_id_type=MESH,
        )
        copy.start()
        sent.append(copy)

    def arrived(dst, ssem, rsem, peer):
        pltpu.make_async_remote_copy(
            src_ref=dst, dst_ref=dst, send_sem=ssem, recv_sem=rsem,
            device_id=peer, device_id_type=MESH,
        ).wait_recv()

    def sigma_at(t, u, cc, owner=None):
        xx = (x, x_same, x_cross, (x + 2) % 4)[t]
        yy = (y + (0, 3, 1, 2)[u]) % 4
        owner = t < 2 if owner is None else owner
        return (s_own if owner else s_oth).at[((xx % 2) * 4 + yy) * 2 + cc]

    def sigma_core(t, u):
        block = sigma_at(t, u, core)
        send(block, block, sc_s.at[t, u], sc_r.at[t, u], c_pair)

    def sigma_y(t):
        block = sigma_at(t, 0, core)
        for d in range(2):
            send(block, block, sy_s.at[t, d], sy_r.at[t, d], y_next[d])

    def sigma_x(u):
        for d in range(2):
            send(sigma_at(0, u, core), sigma_at(0, u, core, d == 0), sx_s.at[u // 3, d], sx_r.at[u // 3, d], x_next[d])

    def far(src, dst, ssem, rsem, peer, d):
        @pl.when(core == d)
        def _():
            pltpu.make_async_remote_copy(
                src_ref=src, dst_ref=dst, send_sem=ssem, recv_sem=rsem,
                device_id=peer, device_id_type=MESH,
            ).start()

    def sigma_first():
        sigma_x(0)
        sigma_y(0)
        sigma_core(0, 0)

    def sigma_x_near(u):
        for d in range(2):
            block = sigma_at(1 + d, u, core)
            arrived(block, sx_s.at[u // 3, d], sx_r.at[u // 3, d], x_next[d])
            far(block, sigma_at(1 + d, u, core, False), sx_s.at[u // 3, 2], sx_r.at[u // 3, 2], x_next[1 - d], d)
            if u == 0:
                sigma_y(1 + d)
            sigma_core(1 + d, u)

    def sigma_x_far(u):
        block = sigma_at(3, u, core)
        arrived(block, sx_s.at[u // 3, 2], sx_r.at[u // 3, 2], x_pair)
        if u == 0:
            sigma_y(3)
        sigma_core(3, u)

    def sigma_y_near(t):
        for d in range(2):
            block = sigma_at(t, 1 + d, core)
            arrived(block, sy_s.at[t, d], sy_r.at[t, d], y_next[d])
            if t == 0:
                far(block, block, sy_s.at[0, 2], sy_r.at[0, 2], y_next[d], d)
            sigma_core(t, 1 + d)

    def sigma_y_far():
        block = sigma_at(0, 3, core)
        arrived(block, sy_s.at[0, 2], sy_r.at[0, 2], y_next[0])
        sigma_x(3)
        sigma_core(0, 3)

    def sigma_ready(n):
        for t in ((2, 3), (0, 1))[n]:
            for u in range(4):
                arrived(sigma_at(t, u, 1 - core), sc_s.at[t, u], sc_r.at[t, u], c_pair)

    def sigma_end():
        block = sigma_at(0, 0, core)
        for ssem, rsem in ((sx_s.at[0, 2], sx_r.at[0, 2]), (sx_s.at[1, 2], sx_r.at[1, 2]), (sy_s.at[0, 2], sy_r.at[0, 2])):
            pltpu.make_async_remote_copy(
                src_ref=block, dst_ref=block, send_sem=ssem, recv_sem=rsem,
                device_id=c_pair, device_id_type=MESH,
            ).wait_send()

    def rows_out(s):
        for i in (8, 6, 10, 4, 12, 2, 14, 7, 9, 5, 11, 3, 13, 1, 15):
            peer = (row + i) % 16
            send(pan.at[s, peer // 2, peer % 2], abuf[s].at[row], a_s.at[s, i], a_r.at[s, i], (peer, col))

    def rows_in(s):
        for i in range(1, 16):
            peer = (row + 16 - i) % 16
            arrived(abuf[s].at[peer], a_s.at[s, i], a_r.at[s, i], (peer, col))

        def take(k, carry):
            block = anc[k, 2 * col + s]
            rows = abuf[s][block].reshape(2, 16, BLK)
            pf[s][0, pl.ds(z, 1), k] = rows[0][None]
            pf[s][1, pl.ds(z, 1), k] = rows[1][None]
            return carry

        lax.fori_loop(0, K, take, 0)

    def ring_start(s):
        for h in range(2):
            for d in range(2):
                z_send(s, h, d, 0)

    def hops(h, d):
        return 4 if d == h else 3

    def piece(s, h, d, hop):
        return pf[s].at[h, (z + (8 - hop if d == 0 else hop)) % 8]

    def z_send(s, h, d, hop):
        block = piece(s, h, d, hop)
        send(block, block, z_s.at[s, h, d, hop], z_r.at[s, h, d, hop], z_next[d])

    def ring(s, hop):
        for h in range(2):
            for d in range(2):
                if hop <= hops(h, d):
                    arrived(piece(s, h, d, hop), z_s.at[s, h, d, hop - 1], z_r.at[s, h, d, hop - 1], z_next[d])
                    if hop < hops(h, d):
                        z_send(s, h, d, hop)

    def pair_out(s):
        send(pan.at[s, :, xh], pbuf.at[s, :, xh], p_s.at[s], p_r.at[s], x_pair)

    def member(s, block):
        here = jnp.int32(0)
        for k in range(K):
            here = here + (anc[k, 2 * col + s] == block).astype(jnp.int32)
        return here.astype(F32)

    def image(s):
        def term(k, carry):
            high, low, s_high, s_low = [], [], [], []
            for i in range(2):
                block = anc[2 * k + i, 2 * col + s]
                p_high, p_low = split(pf[s][:, :, 2 * k + i].reshape(256, BLK))
                high.append(p_high)
                low.append(p_low)
                for rows in (s_oth, s_own):
                    r_high, r_low = split(rows[block])
                    s_high.append(r_high)
                    s_low.append(r_low)
            left = jnp.concatenate(high + low + high, axis=1)
            right = jnp.concatenate(
                [jnp.concatenate(s_high[n::2] + s_high[n::2] + s_low[n::2], axis=0) for n in range(2)], axis=1
            )
            part = jnp.dot(left, right, preferred_element_type=F32)
            for n in range(2):
                cacc[n] = jnp.where(k == 0, 0.0, cacc[n]) + part[:, n * BLK : (n + 1) * BLK]
            return carry

        lax.fori_loop(0, K // 2, term, 0)
        other = cacc[0] * member(s, 2 * z + 1 - xh)
        cacc[0] = other
        cbuf[s] = -other.reshape(2, 8, 16, BLK)
        send(cbuf.at[s], cross.at[s, xh], c_s.at[s], c_r.at[s], x_pair)
        own = cacc[1] * member(s, row)
        cacc[1] = own
        cross[s, pl.ds(xh, 1)] = -own.reshape(1, 2, 8, 16, BLK)

    def image_out(s):
        mine = jnp.zeros((2, 8, 16, BLK), F32)
        for k in range(K):
            mine = mine + pf[s][:, :, k] * (anc[k, 2 * col + s] == 2 * z + 1 - xh).astype(F32)
        for h in range(2):
            pbuf[s, :, pl.ds(xh, 1), 16 * h : 16 * h + 16] = mine[h].reshape(8, 1, 16, BLK)
        arrived(pbuf.at[s, :, 1 - xh], p_s.at[s], p_r.at[s], x_pair)
        over = (((1,), (1,)), ((), ()))
        left, right = [], []
        for rows, parts in ((cacc[1], (p_hi[s], p_lo[s])), (cacc[0], split(pbuf[s].reshape(W, BLK)))):
            high, low = split(rows)
            p_high, p_low = parts
            left += [high, low, high]
            right += [p_high, p_high, p_low]
        product = lax.dot_general(
            jnp.concatenate(left, axis=1), jnp.concatenate(right, axis=1),
            (((1,), (1,)), ((), ())), preferred_element_type=F32,
        )
        dbuf[s] = product.reshape(2, 8, 16, W)
        sums(s, 0)

    def sums(s, hop):
        for h in range(2):
            for d in range(2):
                if hop >= hops(h, d):
                    continue
                away = hops(h, d) - hop
                own = dbuf.at[s, h, (z + (away if d == 0 else 8 - away)) % 8]
                if hop > 0:
                    slot = drz.at[s, h, d, hop - 1]
                    arrived(slot, d_s.at[s, h, d, hop - 1], d_r.at[s, h, d, hop - 1], z_next[d])
                    slot[...] += own[...]
                    own = slot
                send(own, drz.at[s, h, d, hop], d_s.at[s, h, d, hop], d_r.at[s, h, d, hop], z_next[d])

    def sums_end(s):
        for h in range(2):
            total = diag[s, h] + dbuf[s, h, pl.ds(z, 1)].reshape(16, W)
            for d in range(2):
                hop = hops(h, d) - 1
                arrived(drz.at[s, h, d, hop], d_s.at[s, h, d, hop], d_r.at[s, h, d, hop], z_next[d])
                total = total + drz[s, h, d, hop]
            dout[s, h] = total
        arrived(cross.at[s, 1 - xh], c_s.at[s], c_r.at[s], x_pair)

    sigma_first()
    rows_out(0)
    rows_out(1)
    sigma_y_near(0)
    sigma_x_near(0)
    rows_in(0)
    ring_start(0)
    sigma_x_far(0)
    sigma_y_far()
    rows_in(1)
    ring_start(1)
    ring(0,1)
    sigma_y_near(1)
    ring(1,1)
    sigma_x_near(3)
    ring(0,2)
    sigma_y_near(2)
    ring(1,2)
    sigma_x_far(3)
    pair_out(0)
    ring(0,3)
    sigma_y_near(3)
    ring(1,3)
    pair_out(1)
    ring(0,4)
    sigma_ready(1)
    sigma_ready(0)
    image(0)
    image_out(0)
    ring(1,4)
    image(1)
    sums(0,1)
    image_out(1)
    sums(0,2)
    sums(1,1)
    sums(0,3)
    sums(1,2)
    sums(1,3)
    sums_end(0)
    sums_end(1)
    for copy in sent:
        copy.wait_send()
    sigma_end()


def local(sigma_anc, panels, diag_blocks, anc_blocks):
    vmem = pl.BlockSpec(memory_space=pltpu.VMEM)
    dma = pltpu.SemaphoreType.DMA
    cross, dout = pl.pallas_call(
        kernel,
        out_shape=(
            jax.ShapeDtypeStruct((2, 2, 2, 8, 16, BLK), F32),
            jax.ShapeDtypeStruct((2, 2, 16, W), F32),
        ),
        in_specs=[pl.BlockSpec(memory_space=pltpu.SMEM), vmem, vmem, vmem],
        out_specs=(vmem, vmem),
        scratch_shapes=[
            pltpu.VMEM((16, 32, BLK), F32),
            pltpu.VMEM((16, 32, BLK), F32),
            pltpu.VMEM((2, 8, K, 16, BLK), F32),
            pltpu.VMEM((2, 8, K, 16, BLK), F32),
            pltpu.VMEM((NB, BLK, BLK), F32),
            pltpu.VMEM((NB, BLK, BLK), F32),
            pltpu.VMEM((2, 8, 2, 32, BLK), F32),
            pltpu.VMEM((2, 256, BLK), F32),
            pltpu.VMEM((2, 2, 8, 16, BLK), F32),
            pltpu.VMEM((2, 2, 8, 16, W), F32),
            pltpu.VMEM((2, 2, 2, 4, 16, W), F32),
            pltpu.VMEM((2, W, BLK), BF16),
            pltpu.VMEM((2, W, BLK), BF16),
            dma((2, 16)), dma((2, 16)),
            dma((2, 2, 2, 4)), dma((2, 2, 2, 4)),
            dma((2,)), dma((2,)),
            dma((2,)), dma((2,)),
            dma((2, 3)), dma((2, 3)),
            dma((4, 3)), dma((4, 3)),
            dma((4, 4)), dma((4, 4)),
            dma((2, 2, 2, 4)), dma((2, 2, 2, 4)),
        ],
        compiler_params=pltpu.CompilerParams(
            collective_id=0, has_side_effects=True, vmem_limit_bytes=56 << 20
        ),
    )(
        anc_blocks.T,
        sigma_anc,
        panels.reshape(2, 8, 2, 32, BLK),
        diag_blocks.reshape(2, 2, 16, W),
    )
    cross = cross.transpose(0, 3, 1, 2, 4, 5)
    return cross.reshape(2 * W, BLK), dout.reshape(2, 32, W)


def solution(mesh):
    placed = (P("prow", "pcol"), P("pcol", "prow"), P("pcol", "prow", None), P())
    return jax.shard_map(
        local,
        mesh=mesh,
        in_specs=placed,
        out_specs=(P("pcol", "prow"), P("pcol", "prow", None)),
        check_vma=False,
    )
```
